32 devices in a mesh: expert: 32 (over z, y, x, core), hid: 1.
Axes of the slice: x: 2, y: 2, z: 4, core: 2. Of those that a mesh axis runs over, the one named last changes fastest.
Arguments:
- tokens: bfloat16 [4096, 3584], P('expert'), may hold values from -6 to 6
- out_grad: bfloat16 [4096, 3584], P('expert'), may hold values from -4 to 4
- route_ids: int32 [4096, 4], P('expert'), may hold values from 0 to 31, all different within a row; in each aligned block of 128 rows (0 to 127, 128 to 255, ...) at most 24 rows name the same one
- route_gates: float32 [4096, 4], P('expert'), may hold values from 0.1 to 1
- w_gate: bfloat16 [32, 3584, 1024], P('expert', None, 'hid'), may hold values from -0.09375 to 0.09375
- w_up: bfloat16 [32, 3584, 1024], P('expert', None, 'hid'), may hold values from -0.09375 to 0.09375
- w_down: bfloat16 [32, 1024, 3584], P('expert', 'hid'), may hold values from -0.1875 to 0.1875
Outputs:
- token_grad: bfloat16 [4096, 3584], P('expert', 'hid')
- gate_grad: bfloat16 [4096, 4], P('expert')
The draws below stay inside these ranges and needn't reach their ends.
Inputs may be any that keep to these rules, and one draw needn't show every extreme that they name: `route_ids`: each token names 4 different experts. Among the 128 tokens of one index of expert (aligned blocks of rows), no expert is named more than 24 times, a bound that some block reaches.
All inputs are finite; a program needn't handle non-finite values.
Results may differ from the reference program's by a relative error of at most 0.008.
Values may be sent and summed in bfloat16 or wider, within the bound.
A program may use at most 128 MiB of HBM per device.

```python
import math
import jax
import jax.numpy as jnp
import numpy as np
from jax import lax

D = 3584
FF = 1024
TOP_WIN = 4
TOK_DEV = 128
EXPERTS = 32
CAP = 24
TOKENS = 4096
N_EXPERT = 32


def level_of(own_key, extent, split, smallest, high):
    def one(dim, blocks):
        steps = jax.random.uniform(jax.random.fold_in(jax.random.fold_in(own_key, 6), dim), (blocks,), jnp.float32, smallest / len(split), high / len(split))
        return jnp.repeat(jnp.exp(steps), extent[dim] // blocks).reshape((-1,) + (1,) * (len(extent) - dim - 1))

    gain = one(*split[0])
    for cut in split[1:]:
        gain = gain * one(*cut)
    return gain


def assign_block(key, own, number, rows, count, top, most, slope):
    order = jax.random.permutation(key, count)
    heavy_load, common = portions_of(count, rows * top, most, slope, True), portions_of(count, rows * top, most, slope, False)
    places = jnp.arange(count)

    def named(lengths, turn):
        used = int((lengths > 0).sum())
        fixed = max(1, used // 4)
        shifted = fixed + (places - fixed + turn * (used - fixed)) % max(1, count - fixed)
        return jnp.zeros((count,), jnp.int32).at[order[jnp.where(places < fixed, places, shifted)]].set(jnp.asarray(lengths, jnp.int32))

    lengths = jnp.where(number % 4 == 0, named(heavy_load, number // 4), named(common, number - number // 4 - 1))
    mixed = jax.random.permutation(jax.random.fold_in(own, 3), count)
    giver, sink = mixed[0:count // 2 * 2:2], mixed[1:count // 2 * 2:2]
    slack = jnp.minimum(lengths[giver] - 1, most - lengths[sink]) // 2
    slack = jnp.where((giver == order[0]) | (sink == order[0]) | (lengths[sink] == 0), 0, jnp.maximum(slack, 0))
    shifted = jax.random.randint(jax.random.fold_in(own, 4), (count // 2,), 0, 1 << 20) % (slack + 1)
    lengths = lengths.at[giver].add(-shifted).at[sink].add(shifted)
    items = jnp.searchsorted(jnp.cumsum(lengths), jnp.arange(rows * top), side="right").astype(jnp.int32)
    listing = items.reshape(top, rows).T
    listing = listing[jax.random.permutation(jax.random.fold_in(own, 1), rows)]
    turn = jax.random.randint(jax.random.fold_in(own, 2), (rows, 1), 0, top)
    return jnp.take_along_axis(listing, (jnp.arange(top)[None, :] + turn) % top, axis=1)


def portions_of(count, total, reach, slope, full):
    weights = [(1 << 20) // math.isqrt(rank ** slope) + 1 for rank in range(1, count + 1)]
    largest = reach if full else min(reach, max(-(-total // count), total * weights[0] // sum(weights)))
    least = 1 if total - largest >= count - 1 else 0
    given, surplus = [largest] + [least] * (count - 1), total - largest - least * (count - 1)
    while surplus > 0:
        candidates = [i for i in range(1, count) if given[i] < largest] or [i for i in range(1, count) if given[i] < reach]
        pool, budget = sum([weights[i] for i in candidates]), surplus
        for i in candidates:
            more = min(reach - given[i], max(1, budget * weights[i] // pool), surplus)
            given[i] = given[i] + more
            surplus = surplus - more
    return np.array(given)


def centred(rng, dims, spread, most, cuts=(), kind=jnp.bfloat16):
    entries = spread * jax.random.normal(rng, dims, jnp.float32)
    if cuts:
        entries = entries * level_of(rng, dims, cuts, -0.22, 0.18)
    return jnp.clip(entries, -most, most).astype(kind)


def setup_inputs(seed: int = 0) -> dict:
    key_of = jax.random.split(jax.random.key(seed), 8)
    tokens = centred(key_of[0], (TOKENS, D), 1.0, 6.0, ((0, 32),))
    out_grad = centred(key_of[1], (TOKENS, D), 0.5, 4.0, ((0, 32),))
    route_ids_keys = jax.random.split(jax.random.fold_in(key_of[2], 1), TOKENS // TOK_DEV)
    route_ids_turns = jax.random.permutation(jax.random.fold_in(key_of[2], 3), TOKENS // TOK_DEV)
    route_ids = jax.vmap(lambda own, number: assign_block(jax.random.fold_in(key_of[2], 2), own, number, TOK_DEV, EXPERTS, TOP_WIN, CAP, 1))(route_ids_keys, route_ids_turns).reshape((TOKENS, TOP_WIN))
    route_gates = jnp.clip(0.1 + 0.9 * jax.random.uniform(key_of[3], (TOKENS, TOP_WIN), jnp.float32) ** level_of(key_of[3], (TOKENS, TOP_WIN), ((0, 32),), -0.2, 0.2), 0.1, 1.0)
    w_gate = centred(key_of[4], (EXPERTS, D, FF), D ** -0.5, 0.09375, ((0, 32),))
    w_up = centred(key_of[5], (EXPERTS, D, FF), D ** -0.5, 0.09375, ((0, 32),))
    w_down = centred(key_of[6], (EXPERTS, FF, D), FF ** -0.5, 0.1875, ((0, 32),))
    return {"tokens": tokens, "out_grad": out_grad, "route_ids": route_ids, "route_gates": route_gates, "w_gate": w_gate, "w_up": w_up, "w_down": w_down}


def reference(tokens, out_grad, route_ids, route_gates, w_gate, w_up, w_down):
    pair_total = TOKENS * TOP_WIN
    max_rows = N_EXPERT * CAP
    flat_ids = route_ids.reshape(-1).astype(jnp.int32)
    sorted_pairs = jnp.argsort(flat_ids, stable=True).astype(jnp.int32)
    expert_load = jnp.sum((flat_ids[:, None] == jnp.arange(EXPERTS, dtype=jnp.int32)[None, :]).astype(jnp.int32), axis=0)
    load_start = (jnp.cumsum(expert_load) - expert_load).astype(jnp.int32)
    padded_pairs = jnp.concatenate([sorted_pairs, jnp.zeros((max_rows,), jnp.int32)])
    flat_gates = route_gates.reshape(-1).astype(jnp.float32)

    def one_expert(carry, expert):
        grad_acc, score_acc = carry
        pair_idx = lax.dynamic_slice_in_dim(padded_pairs, load_start[expert], max_rows)
        valid = jnp.arange(max_rows, dtype=jnp.int32) < expert_load[expert]
        token_idx = pair_idx // TOP_WIN
        rows_x = tokens[token_idx]
        rows_d = out_grad[token_idx]
        gate_pre = jnp.dot(rows_x, w_gate[expert], preferred_element_type=jnp.float32)
        up_pre = jnp.dot(rows_x, w_up[expert], preferred_element_type=jnp.float32)
        grad_hidden = jnp.dot(rows_d, w_down[expert].T, preferred_element_type=jnp.float32)
        sigma_gate = jax.nn.sigmoid(gate_pre)
        act_gate = gate_pre * sigma_gate
        score = jnp.sum(act_gate * up_pre * grad_hidden, axis=1)
        grad_gate_pre = (grad_hidden * up_pre * sigma_gate * (1.0 + gate_pre * (1.0 - sigma_gate))).astype(jnp.bfloat16)
        grad_up_pre = (grad_hidden * act_gate).astype(jnp.bfloat16)
        pair_grad = (jnp.dot(grad_gate_pre, w_gate[expert].T, preferred_element_type=jnp.float32)
                     + jnp.dot(grad_up_pre, w_up[expert].T, preferred_element_type=jnp.float32)).astype(jnp.bfloat16)
        weighted = pair_grad.astype(jnp.float32) * flat_gates[pair_idx][:, None]
        safe_token = jnp.where(valid, token_idx, TOKENS)
        safe_pair = jnp.where(valid, pair_idx, pair_total)
        grad_acc = grad_acc.at[safe_token].add(weighted, mode="drop")
        score_acc = score_acc.at[safe_pair].set(score, mode="drop")
        return (grad_acc, score_acc), None

    start = (jnp.zeros((TOKENS, D), jnp.float32), jnp.zeros((pair_total,), jnp.float32))
    (grad_acc, score_acc), _ = lax.scan(one_expert, start, jnp.arange(EXPERTS, dtype=jnp.int32))
    token_grad = grad_acc.astype(jnp.bfloat16)
    gate_grad = score_acc.reshape(TOKENS, TOP_WIN).astype(jnp.bfloat16)
    return token_grad, gate_grad
```

```python
import jax
import jax.numpy as jnp
from jax import lax
from jax.sharding import PartitionSpec as P

BF = jnp.bfloat16
F32 = jnp.float32


def place_rows(source, dest_slot, slot_count):
    return jnp.zeros((slot_count, source.shape[1]), source.dtype).at[dest_slot].set(source)


def flat_body(tokens, out_grad, route_ids, route_gates, w_gate, w_up, w_down):
    expert_count = lax.axis_size("expert")
    pair_count = lax.axis_size("hid")
    tok_rows, model_width = tokens.shape
    top_count = route_ids.shape[1]
    capacity = 3 * tok_rows * top_count // (2 * expert_count)
    slot_count = expert_count * capacity
    half_width = model_width // pair_count
    flat_ids = route_ids.reshape(-1)
    one_hot = (flat_ids[:, None] == jnp.arange(expert_count, dtype=jnp.int32)[None, :]).astype(
        jnp.int32
    )
    earlier = jnp.cumsum(one_hot, axis=0) - one_hot
    slot_index = jnp.sum(earlier * one_hot, axis=1)
    dest_slot = flat_ids * capacity + slot_index
    token_of = jnp.arange(tok_rows * top_count, dtype=jnp.int32) // top_count
    send_x = place_rows(tokens[token_of], dest_slot, slot_count).reshape(
        expert_count, capacity, model_width
    )
    send_d = place_rows(out_grad[token_of], dest_slot, slot_count).reshape(
        expert_count, capacity, model_width
    )
    rows_x, rows_d = (
        lax.all_to_all(send_x, "expert", split_axis=0, concat_axis=0, tiled=True),
        lax.all_to_all(send_d, "expert", split_axis=0, concat_axis=0, tiled=True),
    )
    rows_x = rows_x.reshape(slot_count, model_width)
    rows_d = rows_d.reshape(slot_count, model_width)
    grad_part, score_part = expert_math(rows_x, rows_d, w_gate[0], w_up[0], w_down[0])
    grad_share = lax.psum_scatter(grad_part, "hid", scatter_dimension=1, tiled=True).astype(BF)
    score_full = lax.psum(score_part, "hid").astype(BF)
    back_grad, back_score = (
        lax.all_to_all(
            grad_share.reshape(expert_count, capacity, half_width),
            "expert",
            split_axis=0,
            concat_axis=0,
            tiled=True,
        ),
        lax.all_to_all(
            score_full.reshape(expert_count, capacity),
            "expert",
            split_axis=0,
            concat_axis=0,
            tiled=True,
        ),
    )
    picked = back_grad.reshape(slot_count, half_width)[dest_slot]
    picked = picked.reshape(tok_rows, top_count, half_width).astype(F32)
    token_grad = jnp.einsum("tkd,tk->td", picked, route_gates).astype(BF)
    gate_grad = back_score.reshape(slot_count)[dest_slot].reshape(tok_rows, top_count)
    return (token_grad, gate_grad)


def expert_math(rows_x, rows_d, gate_mat, up_mat, down_mat):
    contract_last = (((1,), (1,)), ((), ()))
    gate_pre = jnp.dot(rows_x, gate_mat, preferred_element_type=F32)
    up_pre = jnp.dot(rows_x, up_mat, preferred_element_type=F32)
    grad_hidden = lax.dot_general(rows_d, down_mat, contract_last, preferred_element_type=F32)
    sigma_gate = jax.nn.sigmoid(gate_pre)
    act_gate = gate_pre * sigma_gate
    score_part = jnp.sum(act_gate * up_pre * grad_hidden, axis=1)
    grad_gate_pre = (
        grad_hidden * up_pre * sigma_gate * (1.0 + gate_pre * (1.0 - sigma_gate))
    ).astype(BF)
    grad_up_pre = (grad_hidden * act_gate).astype(BF)
    grad_part = lax.dot_general(
        grad_gate_pre, gate_mat, contract_last, preferred_element_type=F32
    ) + lax.dot_general(grad_up_pre, up_mat, contract_last, preferred_element_type=F32)
    return grad_part, score_part


def slot_masks(ids, experts, capacity):
    tok_rows = ids.shape[-2]
    hit = ids[..., None] == experts
    named = jnp.any(hit, axis=-2).astype(BF)
    before = jnp.tril(jnp.ones((tok_rows, tok_rows), BF), -1)
    rank = jnp.einsum("ut,...te->...eu", before, named, preferred_element_type=F32)
    named = jnp.swapaxes(named, -1, -2) > 0
    slots = jnp.arange(capacity, dtype=F32)
    place = (rank[..., None, :] == slots[:, None]) & named[..., None, :]
    return hit, place


def plane_body(tokens, out_grad, route_ids, route_gates, w_gate, w_up, w_down):
    n = lax.axis_size("expert")
    plane = 8
    layers = n // plane
    tok_rows, width = tokens.shape
    top_count = route_ids.shape[1]
    capacity = 3 * tok_rows * top_count // (2 * n)
    me = lax.axis_index("expert")
    columns = [[z * plane + q for z in range(layers)] for q in range(plane)]
    planes = [[z * plane + q for q in range(plane)] for z in range(layers)]

    def gather_z(a):
        return lax.all_gather(a, "expert", axis_index_groups=columns)

    def swap(a):
        return lax.all_to_all(
            a, "expert", split_axis=0, concat_axis=0, axis_index_groups=planes, tiled=True
        )

    packed = jnp.concatenate([route_ids.astype(F32), route_gates], axis=1)
    packed = gather_z(packed)
    all_x = gather_z(tokens)
    all_d = gather_z(out_grad)
    ids = packed[..., :top_count].astype(jnp.int32)
    gates = packed[..., top_count:]
    local = (me // plane) * plane + jnp.arange(plane, dtype=jnp.int32)
    hit, place = slot_masks(ids, local, capacity)
    gate_of = jnp.einsum("ztke,ztk->zet", hit.astype(F32), gates, precision="highest")
    place_bf = place.astype(BF)
    weights = jnp.where(place, gate_of[:, :, None, :], 0.0)
    high = weights.astype(BF)
    low = (weights - high.astype(F32)).astype(BF)

    def dispatch(rows):
        send = jnp.einsum("zest,ztd->ezsd", place_bf, rows, preferred_element_type=F32).astype(BF)
        return swap(send.reshape(plane, layers * capacity, width)).reshape(-1, width)

    rows_x = dispatch(all_x)
    rows_d = dispatch(all_d)
    grad_part, score = expert_math(rows_x, rows_d, w_gate[0], w_up[0], w_down[0])
    back = swap(grad_part.astype(BF).reshape(plane, layers * capacity, width))
    back = back.reshape(plane, layers, capacity, width)
    both = jnp.concatenate([high, low], axis=1)
    back2 = jnp.concatenate([back, back], axis=0)
    part = jnp.einsum("zest,ezsd->ztd", both, back2, preferred_element_type=F32)
    token_grad = lax.psum_scatter(
        part.astype(BF), "expert", scatter_dimension=0, axis_index_groups=columns, tiled=False
    )
    scores = lax.all_gather(score.astype(BF), "expert").reshape(n, plane, layers, capacity)
    mine = lax.dynamic_index_in_dim(scores, me % plane, 1, keepdims=False)
    mine = lax.dynamic_index_in_dim(mine, me // plane, 1, keepdims=False)
    hit_own, place_own = slot_masks(route_ids, jnp.arange(n, dtype=jnp.int32), capacity)
    by_expert = jnp.einsum("est,es->te", place_own.astype(F32), mine.astype(F32), precision="highest")
    gate_grad = jnp.sum(jnp.where(hit_own, by_expert[:, None, :], 0.0), axis=2).astype(BF)
    return (token_grad, gate_grad)


def solution(mesh):
    n = mesh.shape["expert"]
    flat = mesh.shape["hid"] != 1 or n % 8 != 0
    return jax.shard_map(
        flat_body if flat else plane_body,
        mesh=mesh,
        in_specs=(
            P("expert", None),
            P("expert", None),
            P("expert", None),
            P("expert", None),
            P("expert", None, "hid"),
            P("expert", None, "hid"),
            P("expert", "hid", None),
        ),
        out_specs=(P("expert", "hid"), P("expert", None)),
        check_vma=False,
    )
```

```python
import functools

import jax
import jax.numpy as jnp
from jax import lax
from jax.experimental import pallas as pl
from jax.experimental.pallas import tpu as pltpu
from jax.sharding import PartitionSpec as P

BF = jnp.bfloat16
F32 = jnp.float32
MESH = pl.DeviceIdType.MESH


def place_rows(source, dest_slot, slot_count):
    return jnp.zeros((slot_count, source.shape[1]), source.dtype).at[dest_slot].set(source)


def flat_body(tokens, out_grad, route_ids, route_gates, w_gate, w_up, w_down):
    expert_count = lax.axis_size("expert")
    pair_count = lax.axis_size("hid")
    tok_rows, model_width = tokens.shape
    top_count = route_ids.shape[1]
    capacity = 3 * tok_rows * top_count // (2 * expert_count)
    slot_count = expert_count * capacity
    half_width = model_width // pair_count
    flat_ids = route_ids.reshape(-1)
    one_hot = (flat_ids[:, None] == jnp.arange(expert_count, dtype=jnp.int32)[None, :]).astype(
        jnp.int32
    )
    earlier = jnp.cumsum(one_hot, axis=0) - one_hot
    slot_index = jnp.sum(earlier * one_hot, axis=1)
    dest_slot = flat_ids * capacity + slot_index
    token_of = jnp.arange(tok_rows * top_count, dtype=jnp.int32) // top_count
    send_x = place_rows(tokens[token_of], dest_slot, slot_count).reshape(
        expert_count, capacity, model_width
    )
    send_d = place_rows(out_grad[token_of], dest_slot, slot_count).reshape(
        expert_count, capacity, model_width
    )
    rows_x, rows_d = (
        lax.all_to_all(send_x, "expert", split_axis=0, concat_axis=0, tiled=True),
        lax.all_to_all(send_d, "expert", split_axis=0, concat_axis=0, tiled=True),
    )
    rows_x = rows_x.reshape(slot_count, model_width)
    rows_d = rows_d.reshape(slot_count, model_width)
    grad_part, score_part = expert_math(rows_x, rows_d, w_gate[0], w_up[0], w_down[0])
    grad_share = lax.psum_scatter(grad_part, "hid", scatter_dimension=1, tiled=True).astype(BF)
    score_full = lax.psum(score_part, "hid").astype(BF)
    back_grad, back_score = (
        lax.all_to_all(
            grad_share.reshape(expert_count, capacity, half_width),
            "expert",
            split_axis=0,
            concat_axis=0,
            tiled=True,
        ),
        lax.all_to_all(
            score_full.reshape(expert_count, capacity),
            "expert",
            split_axis=0,
            concat_axis=0,
            tiled=True,
        ),
    )
    picked = back_grad.reshape(slot_count, half_width)[dest_slot]
    picked = picked.reshape(tok_rows, top_count, half_width).astype(F32)
    token_grad = jnp.einsum("tkd,tk->td", picked, route_gates).astype(BF)
    gate_grad = back_score.reshape(slot_count)[dest_slot].reshape(tok_rows, top_count)
    return (token_grad, gate_grad)


def expert_math(rows_x, rows_d, gate_mat, up_mat, down_mat):
    contract_last = (((1,), (1,)), ((), ()))
    gate_pre = jnp.dot(rows_x, gate_mat, preferred_element_type=F32)
    up_pre = jnp.dot(rows_x, up_mat, preferred_element_type=F32)
    grad_hidden = lax.dot_general(rows_d, down_mat, contract_last, preferred_element_type=F32)
    sigma_gate = jax.nn.sigmoid(gate_pre)
    act_gate = gate_pre * sigma_gate
    score_part = jnp.sum(act_gate * up_pre * grad_hidden, axis=1)
    grad_gate_pre = (
        grad_hidden * up_pre * sigma_gate * (1.0 + gate_pre * (1.0 - sigma_gate))
    ).astype(BF)
    grad_up_pre = (grad_hidden * act_gate).astype(BF)
    grad_part = lax.dot_general(
        grad_gate_pre, gate_mat, contract_last, preferred_element_type=F32
    ) + lax.dot_general(grad_up_pre, up_mat, contract_last, preferred_element_type=F32)
    return grad_part, score_part


def fused_kernel(
    layers, plane, rows, cap, width, hidden, top, cw,
    pk_ref, tok_ref, dout_ref, wg_ref, wu_ref, wd_ref, tg_ref, gg_ref,
    pk, ag, snd, rcv, zsnd, zrcv, gz, gzr, sc, scr, pmat, chi, clo,
    acc_g, acc_u, acc_h, ggp, gup, wgs, wus, wds,
    own_sem, ag_ss, ag_rs, snd_ss, rcv_rs, ret_ss, ret_rs, z_ss, z_rs, mis_ss, mis_rs, w_sem,
):
    me = lax.axis_index("expert")
    z = me // plane
    q = me % plane
    per = width // cw
    chunks = 2 * per
    blk = layers * cap
    slots = plane * blk
    toks = layers * rows

    def dev(zz, qq):
        return {"expert": zz * plane + qq}

    def remote(src, dst, ss, rs, who):
        return pltpu.make_async_remote_copy(
            src_ref=src, dst_ref=dst, send_sem=ss, recv_sem=rs, device_id=who, device_id_type=MESH
        )

    def own_copy(c):
        src = tok_ref if c < per else dout_ref
        return pltpu.make_async_copy(
            src.at[:, pl.ds((c % per) * cw, cw)], ag.at[c, z], own_sem.at[c]
        )

    for c in range(chunks):
        own_copy(c).start()

    def w_copies(c, slot):
        at = pl.ds(pl.multiple_of(c * cw, cw), cw)
        return (
            pltpu.make_async_copy(wg_ref.at[at, :], wgs.at[slot], w_sem.at[0, slot]),
            pltpu.make_async_copy(wu_ref.at[at, :], wus.at[slot], w_sem.at[1, slot]),
        )

    def wd_copy(c, slot):
        at = pl.ds(pl.multiple_of(c * cw, cw), cw)
        return pltpu.make_async_copy(wd_ref.at[:, at], wds.at[slot], w_sem.at[2, slot])

    for cp in w_copies(0, 0):
        cp.start()
    wd_copy(0, 0).start()

    barrier = pltpu.get_barrier_semaphore()
    for j in range(1, plane):
        pl.semaphore_signal(barrier, inc=1, device_id=dev(z, (q + j) % plane), device_id_type=MESH)
    for r in range(1, layers):
        pl.semaphore_signal(barrier, inc=1, device_id=dev((z + r) % layers, q), device_id_type=MESH)
    pl.semaphore_wait(barrier, plane - 1 + layers - 1)

    def z_all(src_of, dst, ss, rs):
        for r in range(1, layers):
            remote(src_of(r), dst.at[r], ss, rs, dev((z + r) % layers, q)).start()

    def wait_both(buf, ss, rs):
        done = remote(buf, buf, ss, rs, dev((z + 1) % layers, q))
        done.wait_send()
        done.wait_recv()

    pk[0] = pk_ref[...]
    z_all(lambda r: pk.at[0], pk, mis_ss.at[0], mis_rs.at[0])

    def hop(c, h, way):
        block = z - way * (h - 1)
        d = 0 if way > 0 else 1
        return remote(
            ag.at[c, block], ag.at[c, block], ag_ss.at[c, h - 1, d], ag_rs.at[c, h - 1, d],
            dev(z + way, q),
        )

    def sends(h, way):
        edge = (z + 1 < layers) if way > 0 else (z >= 1)
        has = (z - (h - 1) >= 0) if way > 0 else (z + (h - 1) < layers)
        return jnp.logical_and(edge, has)

    def gets(h, way):
        return (z - h >= 0) if way > 0 else (z + h < layers)

    def start_hop(c, h):
        for way in (1, -1):
            @pl.when(sends(h, way))
            def _():
                hop(c, h, way).start()

    def wait_hop(c, h):
        for way in (1, -1):
            @pl.when(gets(h, way))
            def _():
                block = z - way * h
                d = 0 if way > 0 else 1
                remote(
                    ag.at[c, block], ag.at[c, block], ag_ss.at[c, h - 1, d], ag_rs.at[c, h - 1, d],
                    dev(z - way, q),
                ).wait_recv()

    def plane_send(src, dst, ss, rs, sign):
        for j in range(1, plane):
            remote(src.at[j], dst.at[j], ss, rs, dev(z, (q + sign * j + plane) % plane)).start()

    def group(buf):
        return buf.at[pl.ds(1, plane - 1)]

    def masks():
        wait_both(pk.at[pl.ds(1, layers - 1)], mis_ss.at[0], mis_rs.at[0])
        jj = lax.broadcasted_iota(jnp.int32, (plane, rows), 0)
        expert = (z * plane + (q + jj) % plane).astype(F32)
        lower = lax.broadcasted_iota(jnp.int32, (rows, rows), 0) < lax.broadcasted_iota(
            jnp.int32, (rows, rows), 1
        )
        upper = jnp.where(lower, 1.0, 0.0).astype(BF)
        shape = (plane, layers, cap, rows)
        row_z = lax.broadcasted_iota(jnp.int32, shape, 1)
        row_s = lax.broadcasted_iota(jnp.int32, shape, 2).astype(F32)
        for zs in range(layers):
            info = pk[(z - zs + layers) % layers]
            named = jnp.zeros((plane, rows), F32)
            gate = jnp.zeros((plane, rows), F32)
            for k in range(top):
                same = info[k : k + 1, :] == expert
                named = named + jnp.where(same, 1.0, 0.0)
                gate = gate + jnp.where(same, info[top + k : top + k + 1, :], 0.0)
            rank = jnp.dot(named.astype(BF), upper, preferred_element_type=F32)
            rank = jnp.where(named > 0.5, rank, -1.0)
            full = (row_s == rank[:, None, None, :]) & (row_z == zs)
            one = jnp.where(full, 1.0, 0.0).reshape(slots, rows)
            pmat[:, zs * rows : (zs + 1) * rows] = one.astype(BF)
            wt = jnp.where(full, gate[:, None, None, :], 0.0).reshape(slots, rows).T
            hi = wt.astype(BF)
            chi[zs * rows : (zs + 1) * rows, :] = hi
            clo[zs * rows : (zs + 1) * rows, :] = (wt - hi.astype(F32)).astype(BF)

    masks()
    for c in range(chunks):
        own_copy(c).wait()
    acc_g[...] = jnp.zeros_like(acc_g)
    acc_u[...] = jnp.zeros_like(acc_u)
    acc_h[...] = jnp.zeros_like(acc_h)
    last = (((1,), (1,)), ((), ()))
    tile = 256

    def step(i, _):
        @pl.when(i < chunks)
        def _():
            start_hop(i, 1)

        for h in range(1, layers):
            c = i - h

            @pl.when(jnp.logical_and(c >= 0, c < chunks))
            def _():
                wait_hop(c, h)
                if h < layers - 1:
                    start_hop(c, h + 1)

        c = i - (layers - 1)

        @pl.when(jnp.logical_and(c >= 0, c < chunks))
        def _():
            slot = c % per

            @pl.when(c >= per)
            def _():
                remote(
                    group(snd.at[slot]), group(snd.at[slot]), snd_ss.at[c - per],
                    rcv_rs.at[c - per], dev(z, (q + 1) % plane),
                ).wait_send()

            built = jnp.dot(pmat[...], ag[c].reshape(toks, cw), preferred_element_type=F32)
            built = built.astype(BF).reshape(plane, blk, cw)
            snd[slot] = built
            rcv[c, 0] = built[0]
            plane_send(snd.at[slot], rcv.at[c], snd_ss.at[c], rcv_rs.at[c], 1)

        c2 = i - (layers + 1)

        @pl.when(c2 >= 0)
        def _():
            remote(
                group(rcv.at[c2]), group(rcv.at[c2]), snd_ss.at[c2], rcv_rs.at[c2],
                dev(z, (q + 1) % plane),
            ).wait_recv()
            ws = c2 % 2

            @pl.when(c2 < per)
            def _():
                for cp in w_copies(c2, ws):
                    cp.wait()

                @pl.when(c2 + 1 < per)
                def _():
                    for cp in w_copies(c2 + 1, (c2 + 1) % 2):
                        cp.start()

                @pl.loop(0, hidden // tile)
                def _(t):
                    at = pl.ds(pl.multiple_of(t * tile, tile), tile)
                    xr = rcv[c2].reshape(slots, cw)
                    acc_g[:, at] += jnp.dot(xr, wgs[ws, :, at], preferred_element_type=F32)
                    acc_u[:, at] += jnp.dot(xr, wus[ws, :, at], preferred_element_type=F32)

            @pl.when(c2 >= per)
            def _():
                c3 = c2 - per
                wd_copy(c3, c3 % 2).wait()

                @pl.when(c3 + 1 < per)
                def _():
                    wd_copy(c3 + 1, (c3 + 1) % 2).start()

                @pl.when(c3 == 0)
                def _():
                    for cp in w_copies(0, 0):
                        cp.start()

                @pl.loop(0, hidden // tile)
                def _(t):
                    at = pl.ds(pl.multiple_of(t * tile, tile), tile)
                    dr = rcv[c2].reshape(slots, cw)
                    acc_h[:, at] += lax.dot_general(
                        dr, wds[c3 % 2, at, :], last, preferred_element_type=F32
                    )

        return 0

    lax.fori_loop(0, chunks + layers + 1, step, 0)

    for j in range(plane):
        at = pl.ds(j * blk, blk)
        g, u, d = acc_g[at, :], acc_u[at, :], acc_h[at, :]
        sig = jax.nn.sigmoid(g)
        act = g * sig
        score = jnp.sum(act * u * d, axis=1, keepdims=True)
        sc[j] = jnp.broadcast_to(score, (blk, rows)).astype(BF)
        ggp[at, :] = (d * u * sig * (1.0 + g * (1.0 - sig))).astype(BF)
        gup[at, :] = (d * act).astype(BF)

    scr[0] = sc[0]
    plane_send(sc, scr, mis_ss.at[1], mis_rs.at[1], -1)

    def back(i, _):
        @pl.when(i < per)
        def _():
            ws = i % 2
            for cp in w_copies(i, ws):
                cp.wait()

            @pl.when(i + 1 < per)
            def _():
                for cp in w_copies(i + 1, (i + 1) % 2):
                    cp.start()

            remote(
                group(snd.at[i]), group(snd.at[i]), snd_ss.at[per + i], rcv_rs.at[per + i],
                dev(z, (q + 1) % plane),
            ).wait_send()
            grad = lax.dot_general(ggp[...], wgs[ws], last, preferred_element_type=F32)
            grad = grad + lax.dot_general(gup[...], wus[ws], last, preferred_element_type=F32)
            out = grad.astype(BF).reshape(plane, blk, cw)
            snd[i] = out
            rcv[i, 0] = out[0]
            plane_send(snd.at[i], rcv.at[i], ret_ss.at[i], ret_rs.at[i], -1)

        c = i - 2

        @pl.when(c >= 0)
        def _():
            done = remote(
                group(rcv.at[c]), group(rcv.at[c]), ret_ss.at[c], ret_rs.at[c],
                dev(z, (q + 1) % plane),
            )
            done.wait_send()
            done.wait_recv()
            rr = rcv[c].reshape(slots, cw)
            part = jnp.dot(chi[...], rr, preferred_element_type=F32)
            part = part + jnp.dot(clo[...], rr, preferred_element_type=F32)
            zsnd[c] = part.astype(BF).reshape(layers, rows, cw)
            z_all(lambda r: zsnd.at[c, (z + r) % layers], zrcv.at[c], z_ss.at[c], z_rs.at[c])

        return 0

    lax.fori_loop(0, per + 2, back, 0)

    wait_both(group(scr), mis_ss.at[1], mis_rs.at[1])
    jj = lax.broadcasted_iota(jnp.int32, (plane, rows), 0)
    expert = (z * plane + (q + jj) % plane).astype(F32)
    val = scr[...].astype(F32).reshape(slots, rows)
    for zs in range(layers):
        info = pk[(z - zs + layers) % layers]
        hold = pmat[:, zs * rows : (zs + 1) * rows].astype(F32) * val
        by = jnp.sum(hold.reshape(plane, blk, rows), axis=1)
        parts = [
            jnp.sum(jnp.where(info[k : k + 1, :] == expert, by, 0.0), axis=0, keepdims=True)
            for k in range(top)
        ]
        gz[zs] = jnp.concatenate(parts + [jnp.zeros((8 - top, rows), F32)], axis=0)
    z_all(lambda r: gz.at[(z + r) % layers], gzr, mis_ss.at[2], mis_rs.at[2])

    for c in range(per):
        wait_both(zrcv.at[c, pl.ds(1, layers - 1)], z_ss.at[c], z_rs.at[c])
        total = zsnd[c, z].astype(F32)
        for r in range(1, layers):
            total = total + zrcv[c, r].astype(F32)
        tg_ref[:, c * cw : (c + 1) * cw] = total.astype(BF)

    wait_both(gzr.at[pl.ds(1, layers - 1)], mis_ss.at[2], mis_rs.at[2])
    total = gz[z]
    for r in range(1, layers):
        total = total + gzr[r]
    gg_ref[...] = total

    def drain(c, _):
        for h in range(1, layers):
            for way in (1, -1):
                @pl.when(sends(h, way))
                def _():
                    hop(c, h, way).wait_send()
        return 0

    lax.fori_loop(0, chunks, drain, 0)


def plane_body(tokens, out_grad, route_ids, route_gates, w_gate, w_up, w_down):
    n = lax.axis_size("expert")
    plane = 8
    layers = n // plane
    rows, width = tokens.shape
    hidden = w_gate.shape[2]
    top = route_ids.shape[1]
    cap = 3 * rows * top // (2 * n)
    cw = 512
    per = width // cw
    blk = layers * cap
    slots = plane * blk
    toks = layers * rows
    packed = jnp.concatenate([route_ids.astype(F32), route_gates], axis=1).T
    vm = pl.BlockSpec(memory_space=pltpu.VMEM)
    hbm = pl.BlockSpec(memory_space=pl.ANY)
    dma = pltpu.SemaphoreType.DMA
    token_grad, gates_t = pl.pallas_call(
        functools.partial(fused_kernel, layers, plane, rows, cap, width, hidden, top, cw),
        out_shape=(
            jax.ShapeDtypeStruct((rows, width), BF),
            jax.ShapeDtypeStruct((8, rows), F32),
        ),
        in_specs=[vm, hbm, hbm, hbm, hbm, hbm],
        out_specs=(vm, vm),
        scratch_shapes=[
            pltpu.VMEM((layers, 8, rows), F32),
            pltpu.VMEM((2 * per, layers, rows, cw), BF),
            pltpu.VMEM((per, plane, blk, cw), BF),
            pltpu.VMEM((2 * per, plane, blk, cw), BF),
            pltpu.VMEM((per, layers, rows, cw), BF),
            pltpu.VMEM((per, layers, rows, cw), BF),
            pltpu.VMEM((layers, 8, rows), F32),
            pltpu.VMEM((layers, 8, rows), F32),
            pltpu.VMEM((plane, blk, rows), BF),
            pltpu.VMEM((plane, blk, rows), BF),
            pltpu.VMEM((slots, toks), BF),
            pltpu.VMEM((toks, slots), BF),
            pltpu.VMEM((toks, slots), BF),
            pltpu.VMEM((slots, hidden), F32),
            pltpu.VMEM((slots, hidden), F32),
            pltpu.VMEM((slots, hidden), F32),
            pltpu.VMEM((slots, hidden), BF),
            pltpu.VMEM((slots, hidden), BF),
            pltpu.VMEM((2, cw, hidden), BF),
            pltpu.VMEM((2, cw, hidden), BF),
            pltpu.VMEM((2, hidden, cw), BF),
            dma((2 * per,)),
            dma((2 * per, layers - 1, 2)),
            dma((2 * per, layers - 1, 2)),
            dma((2 * per,)),
            dma((2 * per,)),
            dma((per,)),
            dma((per,)),
            dma((per,)),
            dma((per,)),
            dma((3,)),
            dma((3,)),
            dma((3, 2)),
        ],
        compiler_params=pltpu.CompilerParams(
            collective_id=0, has_side_effects=True, vmem_limit_bytes=64 * 1024 * 1024 - 65536
        ),
        cost_estimate=pl.CostEstimate(
            flops=10 * slots * width * hidden, bytes_accessed=10 * width * hidden, transcendentals=0
        ),
    )(packed, tokens, out_grad, w_gate[0], w_up[0], w_down[0])
    return (token_grad, gates_t[:top].T.astype(BF))


def solution(mesh):
    n = mesh.shape["expert"]
    flat = mesh.shape["hid"] != 1 or n != 32
    return jax.shard_map(
        flat_body if flat else plane_body,
        mesh=mesh,
        in_specs=(
            P("expert", None),
            P("expert", None),
            P("expert", None),
            P("expert", None),
            P("expert", None, "hid"),
            P("expert", None, "hid"),
            P("expert", "hid", None),
        ),
        out_specs=(P("expert", "hid"), P("expert", None)),
        check_vma=False,
    )
```

```python
import functools

import jax
import jax.numpy as jnp
from jax import lax
from jax.experimental import pallas as pl
from jax.experimental.pallas import tpu as pltpu
from jax.sharding import PartitionSpec as P

BF = jnp.bfloat16
F32 = jnp.float32
MESH = pl.DeviceIdType.MESH


def place_rows(source, dest_slot, slot_count):
    return jnp.zeros((slot_count, source.shape[1]), source.dtype).at[dest_slot].set(source)


def flat_body(tokens, out_grad, route_ids, route_gates, w_gate, w_up, w_down):
    expert_count = lax.axis_size("expert")
    pair_count = lax.axis_size("hid")
    tok_rows, model_width = tokens.shape
    top_count = route_ids.shape[1]
    capacity = 3 * tok_rows * top_count // (2 * expert_count)
    slot_count = expert_count * capacity
    half_width = model_width // pair_count
    flat_ids = route_ids.reshape(-1)
    one_hot = (flat_ids[:, None] == jnp.arange(expert_count, dtype=jnp.int32)[None, :]).astype(
        jnp.int32
    )
    earlier = jnp.cumsum(one_hot, axis=0) - one_hot
    slot_index = jnp.sum(earlier * one_hot, axis=1)
    dest_slot = flat_ids * capacity + slot_index
    token_of = jnp.arange(tok_rows * top_count, dtype=jnp.int32) // top_count
    send_x = place_rows(tokens[token_of], dest_slot, slot_count).reshape(
        expert_count, capacity, model_width
    )
    send_d = place_rows(out_grad[token_of], dest_slot, slot_count).reshape(
        expert_count, capacity, model_width
    )
    rows_x, rows_d = (
        lax.all_to_all(send_x, "expert", split_axis=0, concat_axis=0, tiled=True),
        lax.all_to_all(send_d, "expert", split_axis=0, concat_axis=0, tiled=True),
    )
    rows_x = rows_x.reshape(slot_count, model_width)
    rows_d = rows_d.reshape(slot_count, model_width)
    grad_part, score_part = expert_math(rows_x, rows_d, w_gate[0], w_up[0], w_down[0])
    grad_share = lax.psum_scatter(grad_part, "hid", scatter_dimension=1, tiled=True).astype(BF)
    score_full = lax.psum(score_part, "hid").astype(BF)
    back_grad, back_score = (
        lax.all_to_all(
            grad_share.reshape(expert_count, capacity, half_width),
            "expert",
            split_axis=0,
            concat_axis=0,
            tiled=True,
        ),
        lax.all_to_all(
            score_full.reshape(expert_count, capacity),
            "expert",
            split_axis=0,
            concat_axis=0,
            tiled=True,
        ),
    )
    picked = back_grad.reshape(slot_count, half_width)[dest_slot]
    picked = picked.reshape(tok_rows, top_count, half_width).astype(F32)
    token_grad = jnp.einsum("tkd,tk->td", picked, route_gates).astype(BF)
    gate_grad = back_score.reshape(slot_count)[dest_slot].reshape(tok_rows, top_count)
    return (token_grad, gate_grad)


def expert_math(rows_x, rows_d, gate_mat, up_mat, down_mat):
    contract_last = (((1,), (1,)), ((), ()))
    gate_pre = jnp.dot(rows_x, gate_mat, preferred_element_type=F32)
    up_pre = jnp.dot(rows_x, up_mat, preferred_element_type=F32)
    grad_hidden = lax.dot_general(rows_d, down_mat, contract_last, preferred_element_type=F32)
    sigma_gate = jax.nn.sigmoid(gate_pre)
    act_gate = gate_pre * sigma_gate
    score_part = jnp.sum(act_gate * up_pre * grad_hidden, axis=1)
    grad_gate_pre = (
        grad_hidden * up_pre * sigma_gate * (1.0 + gate_pre * (1.0 - sigma_gate))
    ).astype(BF)
    grad_up_pre = (grad_hidden * act_gate).astype(BF)
    grad_part = lax.dot_general(
        grad_gate_pre, gate_mat, contract_last, preferred_element_type=F32
    ) + lax.dot_general(grad_up_pre, up_mat, contract_last, preferred_element_type=F32)
    return grad_part, score_part


def fused_kernel(
    layers, plane, rows, cap, width, hidden, top, cw,
    pk_ref, tok_ref, dout_ref, wg_ref, wu_ref, wd_ref, tg_ref, gg_ref,
    pk, ag, snd, rcv, zsnd, zrcv, gz, gzr, sc, scr, pmat, chi, clo,
    acc_g, acc_u, acc_h, ggp, gup, wgs, wus, wds,
    own_sem, ag_ss, ag_rs, snd_ss, rcv_rs, ret_ss, ret_rs, z_ss, z_rs, mis_ss, mis_rs, w_sem,
):
    me = lax.axis_index("expert")
    z = me // plane
    q = me % plane
    per = width // cw
    chunks = 2 * per
    blk = layers * cap
    slots = plane * blk
    toks = layers * rows

    def dev(zz, qq):
        return {"expert": zz * plane + qq}

    def remote(src, dst, ss, rs, who):
        return pltpu.make_async_remote_copy(
            src_ref=src, dst_ref=dst, send_sem=ss, recv_sem=rs, device_id=who, device_id_type=MESH
        )

    def own_copy(c):
        src = tok_ref if c < per else dout_ref
        return pltpu.make_async_copy(
            src.at[:, pl.ds((c % per) * cw, cw)], ag.at[c, z], own_sem.at[c]
        )

    for c in range(chunks):
        own_copy(c).start()

    def w_copies(c, slot):
        at = pl.ds(pl.multiple_of(c * cw, cw), cw)
        return (
            pltpu.make_async_copy(wg_ref.at[at, :], wgs.at[slot], w_sem.at[0, slot]),
            pltpu.make_async_copy(wu_ref.at[at, :], wus.at[slot], w_sem.at[1, slot]),
        )

    def wd_copy(c, slot):
        at = pl.ds(pl.multiple_of(c * cw, cw), cw)
        return pltpu.make_async_copy(wd_ref.at[:, at], wds.at[slot], w_sem.at[2, slot])

    for cp in w_copies(0, 0):
        cp.start()
    wd_copy(0, 0).start()

    barrier = pltpu.get_barrier_semaphore()
    for j in range(1, plane):
        pl.semaphore_signal(barrier, inc=1, device_id=dev(z, (q + j) % plane), device_id_type=MESH)
    for r in range(1, layers):
        pl.semaphore_signal(barrier, inc=1, device_id=dev((z + r) % layers, q), device_id_type=MESH)
    pl.semaphore_wait(barrier, plane - 1 + layers - 1)

    def z_all(src_of, dst, ss, rs):
        for r in range(1, layers):
            remote(src_of(r), dst.at[r], ss, rs, dev((z + r) % layers, q)).start()

    def wait_both(buf, ss, rs):
        done = remote(buf, buf, ss, rs, dev((z + 1) % layers, q))
        done.wait_send()
        done.wait_recv()

    pk[0] = pk_ref[...]
    z_all(lambda r: pk.at[0], pk, mis_ss.at[0], mis_rs.at[0])

    def hop(c, h, way):
        block = z - way * (h - 1)
        d = 0 if way > 0 else 1
        return remote(
            ag.at[c, block], ag.at[c, block], ag_ss.at[c, h - 1, d], ag_rs.at[c, h - 1, d],
            dev(z + way, q),
        )

    def sends(h, way):
        edge = (z + 1 < layers) if way > 0 else (z >= 1)
        has = (z - (h - 1) >= 0) if way > 0 else (z + (h - 1) < layers)
        return jnp.logical_and(edge, has)

    def gets(h, way):
        return (z - h >= 0) if way > 0 else (z + h < layers)

    def start_hop(c, h):
        for way in (1, -1):
            @pl.when(sends(h, way))
            def _():
                hop(c, h, way).start()

    def wait_hop(c, h):
        for way in (1, -1):
            @pl.when(gets(h, way))
            def _():
                block = z - way * h
                d = 0 if way > 0 else 1
                remote(
                    ag.at[c, block], ag.at[c, block], ag_ss.at[c, h - 1, d], ag_rs.at[c, h - 1, d],
                    dev(z - way, q),
                ).wait_recv()

    def plane_send(src, dst, ss, rs, sign):
        for j in range(1, plane):
            remote(src.at[j], dst.at[j], ss, rs, dev(z, (q + sign * j + plane) % plane)).start()

    def group(buf):
        return buf.at[pl.ds(1, plane - 1)]

    def masks():
        wait_both(pk.at[pl.ds(1, layers - 1)], mis_ss.at[0], mis_rs.at[0])
        jj = lax.broadcasted_iota(jnp.int32, (plane, rows), 0)
        expert = (z * plane + (q + jj) % plane).astype(F32)
        lower = lax.broadcasted_iota(jnp.int32, (rows, rows), 0) < lax.broadcasted_iota(
            jnp.int32, (rows, rows), 1
        )
        upper = jnp.where(lower, 1.0, 0.0).astype(BF)
        shape = (plane, layers, cap, rows)
        row_z = lax.broadcasted_iota(jnp.int32, shape, 1)
        row_s = lax.broadcasted_iota(jnp.int32, shape, 2).astype(F32)
        for zs in range(layers):
            info = pk[(z - zs + layers) % layers]
            named = jnp.zeros((plane, rows), F32)
            gate = jnp.zeros((plane, rows), F32)
            for k in range(top):
                same = info[k : k + 1, :] == expert
                named = named + jnp.where(same, 1.0, 0.0)
                gate = gate + jnp.where(same, info[top + k : top + k + 1, :], 0.0)
            rank = jnp.dot(named.astype(BF), upper, preferred_element_type=F32)
            rank = jnp.where(named > 0.5, rank, -1.0)
            full = (row_s == rank[:, None, None, :]) & (row_z == zs)
            one = jnp.where(full, 1.0, 0.0).reshape(slots, rows)
            pmat[:, zs * rows : (zs + 1) * rows] = one.astype(BF)
            wt = jnp.where(full, gate[:, None, None, :], 0.0).reshape(slots, rows).T
            hi = wt.astype(BF)
            chi[zs * rows : (zs + 1) * rows, :] = hi
            clo[zs * rows : (zs + 1) * rows, :] = (wt - hi.astype(F32)).astype(BF)

    for c in range(chunks):
        own_copy(c).wait()
    start_hop(0, 1)
    start_hop(1, 1)
    masks()
    acc_g[...] = jnp.zeros_like(acc_g)
    acc_u[...] = jnp.zeros_like(acc_u)
    acc_h[...] = jnp.zeros_like(acc_h)
    last = (((1,), (1,)), ((), ()))
    tile = 256

    def step(i, _):
        @pl.when(jnp.logical_and(i >= 2, i < chunks))
        def _():
            start_hop(i, 1)

        for h in range(1, layers):
            c = i - h

            @pl.when(jnp.logical_and(c >= 0, c < chunks))
            def _():
                wait_hop(c, h)
                if h < layers - 1:
                    start_hop(c, h + 1)

        c = i - (layers - 1)

        @pl.when(jnp.logical_and(c >= 0, c < chunks))
        def _():
            slot = c % per

            @pl.when(c >= per)
            def _():
                remote(
                    group(snd.at[slot]), group(snd.at[slot]), snd_ss.at[c - per],
                    rcv_rs.at[c - per], dev(z, (q + 1) % plane),
                ).wait_send()

            built = jnp.dot(pmat[...], ag[c].reshape(toks, cw), preferred_element_type=F32)
            built = built.astype(BF).reshape(plane, blk, cw)
            snd[slot] = built
            rcv[c, 0] = built[0]
            plane_send(snd.at[slot], rcv.at[c], snd_ss.at[c], rcv_rs.at[c], 1)

        c2 = i - (layers + 1)

        @pl.when(c2 >= 0)
        def _():
            remote(
                group(rcv.at[c2]), group(rcv.at[c2]), snd_ss.at[c2], rcv_rs.at[c2],
                dev(z, (q + 1) % plane),
            ).wait_recv()
            ws = c2 % 2

            @pl.when(c2 < per)
            def _():
                for cp in w_copies(c2, ws):
                    cp.wait()

                @pl.when(c2 + 1 < per)
                def _():
                    for cp in w_copies(c2 + 1, (c2 + 1) % 2):
                        cp.start()

                @pl.loop(0, hidden // tile)
                def _(t):
                    at = pl.ds(pl.multiple_of(t * tile, tile), tile)
                    xr = rcv[c2].reshape(slots, cw)
                    acc_g[:, at] += jnp.dot(xr, wgs[ws, :, at], preferred_element_type=F32)
                    acc_u[:, at] += jnp.dot(xr, wus[ws, :, at], preferred_element_type=F32)

            @pl.when(c2 >= per)
            def _():
                c3 = c2 - per
                wd_copy(c3, c3 % 2).wait()

                @pl.when(c3 + 1 < per)
                def _():
                    wd_copy(c3 + 1, (c3 + 1) % 2).start()

                @pl.when(c3 == 0)
                def _():
                    for cp in w_copies(0, 0):
                        cp.start()

                @pl.loop(0, hidden // tile)
                def _(t):
                    at = pl.ds(pl.multiple_of(t * tile, tile), tile)
                    dr = rcv[c2].reshape(slots, cw)
                    acc_h[:, at] += lax.dot_general(
                        dr, wds[c3 % 2, at, :], last, preferred_element_type=F32
                    )

        return 0

    lax.fori_loop(0, chunks + layers + 1, step, 0)

    for j in range(plane):
        at = pl.ds(j * blk, blk)
        g, u, d = acc_g[at, :], acc_u[at, :], acc_h[at, :]
        sig = jax.nn.sigmoid(g)
        act = g * sig
        score = jnp.sum(act * u * d, axis=1, keepdims=True)
        sc[j] = jnp.broadcast_to(score, (blk, rows)).astype(BF)
        ggp[at, :] = (d * u * sig * (1.0 + g * (1.0 - sig))).astype(BF)
        gup[at, :] = (d * act).astype(BF)

    scr[0] = sc[0]
    plane_send(sc, scr, mis_ss.at[1], mis_rs.at[1], -1)

    outer = jnp.logical_or(z == 0, z == layers - 1)
    inner = jnp.logical_not(outer)
    beside = z + 1 - 2 * (z % 2)
    across, far = layers - 1 - z, layers - 1 - beside

    def to_layer(c, block, slot, who, turn):
        return remote(
            zsnd.at[c, block], zrcv.at[c, slot], z_ss.at[c, turn], z_rs.at[c, turn], dev(who, q)
        )

    def landed(c, start, count, turn):
        some = zrcv.at[c, pl.ds(start, count)]
        return remote(some, some, z_ss.at[c, turn], z_rs.at[c, turn], dev(beside, q))

    def first_hop(c):
        to_layer(c, beside, 0, beside, 0).start()

        @pl.when(outer)
        def _():
            to_layer(c, far, 1, beside, 0).start()
            to_layer(c, across, 2, beside, 0).start()

    def second_hop(c):
        landed(c, 0, 3, 0).wait_recv()
        for block, slot in ((across, 1), (far, 2)):
            both = zsnd[c, block].astype(F32) + zrcv[c, slot].astype(F32)
            zsnd[c, block] = both.astype(BF)
            to_layer(c, block, 3, block, 1).start()

    def back(i, _):
        @pl.when(i < per)
        def _():
            ws = i % 2
            for cp in w_copies(i, ws):
                cp.wait()

            @pl.when(i + 1 < per)
            def _():
                for cp in w_copies(i + 1, (i + 1) % 2):
                    cp.start()

            remote(
                group(snd.at[i]), group(snd.at[i]), snd_ss.at[per + i], rcv_rs.at[per + i],
                dev(z, (q + 1) % plane),
            ).wait_send()
            grad = lax.dot_general(ggp[...], wgs[ws], last, preferred_element_type=F32)
            grad = grad + lax.dot_general(gup[...], wus[ws], last, preferred_element_type=F32)
            out = grad.astype(BF).reshape(plane, blk, cw)
            snd[i] = out
            rcv[i, 0] = out[0]
            plane_send(snd.at[i], rcv.at[i], ret_ss.at[i], ret_rs.at[i], -1)

        c = i - 2

        @pl.when(jnp.logical_and(c >= 0, c < per))
        def _():
            done = remote(
                group(rcv.at[c]), group(rcv.at[c]), ret_ss.at[c], ret_rs.at[c],
                dev(z, (q + 1) % plane),
            )
            done.wait_send()
            done.wait_recv()
            rr = rcv[c].reshape(slots, cw)
            part = jnp.dot(chi[...], rr, preferred_element_type=F32)
            part = part + jnp.dot(clo[...], rr, preferred_element_type=F32)
            zsnd[c] = part.astype(BF).reshape(layers, rows, cw)
            first_hop(c)

        b = i - 3

        @pl.when(jnp.logical_and(b >= 0, inner))
        def _():
            second_hop(b)

        return 0

    lax.fori_loop(0, per + 3, back, 0)

    wait_both(group(scr), mis_ss.at[1], mis_rs.at[1])
    jj = lax.broadcasted_iota(jnp.int32, (plane, rows), 0)
    expert = (z * plane + (q + jj) % plane).astype(F32)
    val = scr[...].astype(F32).reshape(slots, rows)
    for zs in range(layers):
        info = pk[(z - zs + layers) % layers]
        hold = pmat[:, zs * rows : (zs + 1) * rows].astype(F32) * val
        by = jnp.sum(hold.reshape(plane, blk, rows), axis=1)
        parts = [
            jnp.sum(jnp.where(info[k : k + 1, :] == expert, by, 0.0), axis=0, keepdims=True)
            for k in range(top)
        ]
        gz[zs] = jnp.concatenate(parts + [jnp.zeros((8 - top, rows), F32)], axis=0)
    z_all(lambda r: gz.at[(z + r) % layers], gzr, mis_ss.at[2], mis_rs.at[2])

    for c in range(per):
        @pl.when(outer)
        def _():
            landed(c, 0, 1, 0).wait_recv()
            landed(c, 0, 3, 0).wait_send()

        @pl.when(inner)
        def _():
            landed(c, 0, 1, 0).wait_send()
            landed(c, 0, 2, 1).wait_send()

        landed(c, 3, 1, 1).wait_recv()
        total = zsnd[c, z].astype(F32) + zrcv[c, 0].astype(F32) + zrcv[c, 3].astype(F32)
        tg_ref[:, c * cw : (c + 1) * cw] = total.astype(BF)

    wait_both(gzr.at[pl.ds(1, layers - 1)], mis_ss.at[2], mis_rs.at[2])
    total = gz[z]
    for r in range(1, layers):
        total = total + gzr[r]
    gg_ref[...] = total

    def drain(c, _):
        for h in range(1, layers):
            for way in (1, -1):
                @pl.when(sends(h, way))
                def _():
                    hop(c, h, way).wait_send()
        return 0

    lax.fori_loop(0, chunks, drain, 0)


def plane_body(tokens, out_grad, route_ids, route_gates, w_gate, w_up, w_down):
    n = lax.axis_size("expert")
    plane = 8
    layers = n // plane
    rows, width = tokens.shape
    hidden = w_gate.shape[2]
    top = route_ids.shape[1]
    cap = 3 * rows * top // (2 * n)
    cw = 512
    per = width // cw
    blk = layers * cap
    slots = plane * blk
    toks = layers * rows
    packed = jnp.concatenate([route_ids.astype(F32), route_gates], axis=1).T
    vm = pl.BlockSpec(memory_space=pltpu.VMEM)
    hbm = pl.BlockSpec(memory_space=pl.ANY)
    dma = pltpu.SemaphoreType.DMA
    token_grad, gates_t = pl.pallas_call(
        functools.partial(fused_kernel, layers, plane, rows, cap, width, hidden, top, cw),
        out_shape=(
            jax.ShapeDtypeStruct((rows, width), BF),
            jax.ShapeDtypeStruct((8, rows), F32),
        ),
        in_specs=[vm, hbm, hbm, hbm, hbm, hbm],
        out_specs=(vm, vm),
        scratch_shapes=[
            pltpu.VMEM((layers, 8, rows), F32),
            pltpu.VMEM((2 * per, layers, rows, cw), BF),
            pltpu.VMEM((per, plane, blk, cw), BF),
            pltpu.VMEM((2 * per, plane, blk, cw), BF),
            pltpu.VMEM((per, layers, rows, cw), BF),
            pltpu.VMEM((per, layers, rows, cw), BF),
            pltpu.VMEM((layers, 8, rows), F32),
            pltpu.VMEM((layers, 8, rows), F32),
            pltpu.VMEM((plane, blk, rows), BF),
            pltpu.VMEM((plane, blk, rows), BF),
            pltpu.VMEM((slots, toks), BF),
            pltpu.VMEM((toks, slots), BF),
            pltpu.VMEM((toks, slots), BF),
            pltpu.VMEM((slots, hidden), F32),
            pltpu.VMEM((slots, hidden), F32),
            pltpu.VMEM((slots, hidden), F32),
            pltpu.VMEM((slots, hidden), BF),
            pltpu.VMEM((slots, hidden), BF),
            pltpu.VMEM((2, cw, hidden), BF),
            pltpu.VMEM((2, cw, hidden), BF),
            pltpu.VMEM((2, hidden, cw), BF),
            dma((2 * per,)),
            dma((2 * per, layers - 1, 2)),
            dma((2 * per, layers - 1, 2)),
            dma((2 * per,)),
            dma((2 * per,)),
            dma((per,)),
            dma((per,)),
            dma((per, 2)),
            dma((per, 2)),
            dma((3,)),
            dma((3,)),
            dma((3, 2)),
        ],
        compiler_params=pltpu.CompilerParams(
            collective_id=0, has_side_effects=True, vmem_limit_bytes=64 * 1024 * 1024 - 65536
        ),
        cost_estimate=pl.CostEstimate(
            flops=10 * slots * width * hidden, bytes_accessed=10 * width * hidden, transcendentals=0
        ),
    )(packed, tokens, out_grad, w_gate[0], w_up[0], w_down[0])
    return (token_grad, gates_t[:top].T.astype(BF))


def solution(mesh):
    n = mesh.shape["expert"]
    flat = mesh.shape["hid"] != 1 or n != 32
    return jax.shard_map(
        flat_body if flat else plane_body,
        mesh=mesh,
        in_specs=(
            P("expert", None),
            P("expert", None),
            P("expert", None),
            P("expert", None),
            P("expert", None, "hid"),
            P("expert", None, "hid"),
            P("expert", "hid", None),
        ),
        out_specs=(P("expert", "hid"), P("expert", None)),
        check_vma=False,
    )
```

```python
import functools

import jax
import jax.numpy as jnp
from jax import lax
from jax.experimental import pallas as pl
from jax.experimental.pallas import tpu as pltpu
from jax.sharding import PartitionSpec as P

BF = jnp.bfloat16
F32 = jnp.float32
MESH = pl.DeviceIdType.MESH


def place_rows(source, dest_slot, slot_count):
    return jnp.zeros((slot_count, source.shape[1]), source.dtype).at[dest_slot].set(source)


def flat_body(tokens, out_grad, route_ids, route_gates, w_gate, w_up, w_down):
    expert_count = lax.axis_size("expert")
    pair_count = lax.axis_size("hid")
    tok_rows, model_width = tokens.shape
    top_count = route_ids.shape[1]
    capacity = 3 * tok_rows * top_count // (2 * expert_count)
    slot_count = expert_count * capacity
    half_width = model_width // pair_count
    flat_ids = route_ids.reshape(-1)
    one_hot = (flat_ids[:, None] == jnp.arange(expert_count, dtype=jnp.int32)[None, :]).astype(
        jnp.int32
    )
    earlier = jnp.cumsum(one_hot, axis=0) - one_hot
    slot_index = jnp.sum(earlier * one_hot, axis=1)
    dest_slot = flat_ids * capacity + slot_index
    token_of = jnp.arange(tok_rows * top_count, dtype=jnp.int32) // top_count
    send_x = place_rows(tokens[token_of], dest_slot, slot_count).reshape(
        expert_count, capacity, model_width
    )
    send_d = place_rows(out_grad[token_of], dest_slot, slot_count).reshape(
        expert_count, capacity, model_width
    )
    rows_x, rows_d = (
        lax.all_to_all(send_x, "expert", split_axis=0, concat_axis=0, tiled=True),
        lax.all_to_all(send_d, "expert", split_axis=0, concat_axis=0, tiled=True),
    )
    rows_x = rows_x.reshape(slot_count, model_width)
    rows_d = rows_d.reshape(slot_count, model_width)
    grad_part, score_part = expert_math(rows_x, rows_d, w_gate[0], w_up[0], w_down[0])
    grad_share = lax.psum_scatter(grad_part, "hid", scatter_dimension=1, tiled=True).astype(BF)
    score_full = lax.psum(score_part, "hid").astype(BF)
    back_grad, back_score = (
        lax.all_to_all(
            grad_share.reshape(expert_count, capacity, half_width),
            "expert",
            split_axis=0,
            concat_axis=0,
            tiled=True,
        ),
        lax.all_to_all(
            score_full.reshape(expert_count, capacity),
            "expert",
            split_axis=0,
            concat_axis=0,
            tiled=True,
        ),
    )
    picked = back_grad.reshape(slot_count, half_width)[dest_slot]
    picked = picked.reshape(tok_rows, top_count, half_width).astype(F32)
    token_grad = jnp.einsum("tkd,tk->td", picked, route_gates).astype(BF)
    gate_grad = back_score.reshape(slot_count)[dest_slot].reshape(tok_rows, top_count)
    return (token_grad, gate_grad)


def expert_math(rows_x, rows_d, gate_mat, up_mat, down_mat):
    contract_last = (((1,), (1,)), ((), ()))
    gate_pre = jnp.dot(rows_x, gate_mat, preferred_element_type=F32)
    up_pre = jnp.dot(rows_x, up_mat, preferred_element_type=F32)
    grad_hidden = lax.dot_general(rows_d, down_mat, contract_last, preferred_element_type=F32)
    sigma_gate = jax.nn.sigmoid(gate_pre)
    act_gate = gate_pre * sigma_gate
    score_part = jnp.sum(act_gate * up_pre * grad_hidden, axis=1)
    grad_gate_pre = (
        grad_hidden * up_pre * sigma_gate * (1.0 + gate_pre * (1.0 - sigma_gate))
    ).astype(BF)
    grad_up_pre = (grad_hidden * act_gate).astype(BF)
    grad_part = lax.dot_general(
        grad_gate_pre, gate_mat, contract_last, preferred_element_type=F32
    ) + lax.dot_general(grad_up_pre, up_mat, contract_last, preferred_element_type=F32)
    return grad_part, score_part


def fused_kernel(
    layers, plane, rows, cap, width, hidden, top, cw,
    pk_ref, tok_ref, dout_ref, wg_ref, wu_ref, wd_ref, tg_ref, gg_ref,
    pk, ag, snd, rcv, zsnd, zrcv, gz, gzr, sc, scr, pmat, chi, clo,
    acc_g, acc_u, acc_h, ggp, gup, wgs, wus, wds,
    own_sem, ag_ss, ag_rs, snd_ss, rcv_rs, ret_ss, ret_rs, z_ss, z_rs, mis_ss, mis_rs, w_sem,
):
    me = lax.axis_index("expert")
    z = me // plane
    q = me % plane
    per = width // cw
    chunks = 2 * per
    blk = layers * cap
    slots = plane * blk
    toks = layers * rows

    def dev(zz, qq):
        return {"expert": zz * plane + qq}

    def remote(src, dst, ss, rs, who):
        return pltpu.make_async_remote_copy(
            src_ref=src, dst_ref=dst, send_sem=ss, recv_sem=rs, device_id=who, device_id_type=MESH
        )

    def own_copy(c):
        src = tok_ref if c < per else dout_ref
        return pltpu.make_async_copy(
            src.at[:, pl.ds((c % per) * cw, cw)], ag.at[c, z], own_sem.at[c]
        )

    for c in range(chunks):
        own_copy(c).start()

    def w_copies(c, slot):
        at = pl.ds(pl.multiple_of(c * cw, cw), cw)
        return (
            pltpu.make_async_copy(wg_ref.at[at, :], wgs.at[slot], w_sem.at[0, slot]),
            pltpu.make_async_copy(wu_ref.at[at, :], wus.at[slot], w_sem.at[1, slot]),
        )

    def wd_copy(c, slot):
        at = pl.ds(pl.multiple_of(c * cw, cw), cw)
        return pltpu.make_async_copy(wd_ref.at[:, at], wds.at[slot], w_sem.at[2, slot])

    for cp in w_copies(0, 0):
        cp.start()
    wd_copy(0, 0).start()

    barrier = pltpu.get_barrier_semaphore()
    for j in range(1, plane):
        pl.semaphore_signal(barrier, inc=1, device_id=dev(z, (q + j) % plane), device_id_type=MESH)
    for r in range(1, layers):
        pl.semaphore_signal(barrier, inc=1, device_id=dev((z + r) % layers, q), device_id_type=MESH)
    pl.semaphore_wait(barrier, plane - 1 + layers - 1)

    def z_all(src_of, dst, ss, rs):
        for r in range(1, layers):
            remote(src_of(r), dst.at[r], ss, rs, dev((z + r) % layers, q)).start()

    def wait_both(buf, ss, rs):
        done = remote(buf, buf, ss, rs, dev((z + 1) % layers, q))
        done.wait_send()
        done.wait_recv()

    pk[0] = pk_ref[...]
    z_all(lambda r: pk.at[0], pk, mis_ss.at[0], mis_rs.at[0])

    def hop(c, h, way):
        block = z - way * (h - 1)
        d = 0 if way > 0 else 1
        return remote(
            ag.at[c, block], ag.at[c, block], ag_ss.at[c, h - 1, d], ag_rs.at[c, h - 1, d],
            dev(z + way, q),
        )

    def sends(h, way):
        edge = (z + 1 < layers) if way > 0 else (z >= 1)
        has = (z - (h - 1) >= 0) if way > 0 else (z + (h - 1) < layers)
        return jnp.logical_and(edge, has)

    def gets(h, way):
        return (z - h >= 0) if way > 0 else (z + h < layers)

    def start_hop(c, h):
        for way in (1, -1):
            @pl.when(sends(h, way))
            def _():
                hop(c, h, way).start()

    def wait_hop(c, h):
        for way in (1, -1):
            @pl.when(gets(h, way))
            def _():
                block = z - way * h
                d = 0 if way > 0 else 1
                remote(
                    ag.at[c, block], ag.at[c, block], ag_ss.at[c, h - 1, d], ag_rs.at[c, h - 1, d],
                    dev(z - way, q),
                ).wait_recv()

    def plane_send(src, dst, ss, rs, sign):
        for j in range(1, plane):
            remote(src.at[j], dst.at[j], ss, rs, dev(z, (q + sign * j + plane) % plane)).start()

    def group(buf):
        return buf.at[pl.ds(1, plane - 1)]

    def masks():
        wait_both(pk.at[pl.ds(1, layers - 1)], mis_ss.at[0], mis_rs.at[0])
        jj = lax.broadcasted_iota(jnp.int32, (plane, rows), 0)
        expert = (z * plane + (q + jj) % plane).astype(F32)
        lower = lax.broadcasted_iota(jnp.int32, (rows, rows), 0) < lax.broadcasted_iota(
            jnp.int32, (rows, rows), 1
        )
        upper = jnp.where(lower, 1.0, 0.0).astype(BF)
        shape = (plane, layers, cap, rows)
        row_z = lax.broadcasted_iota(jnp.int32, shape, 1)
        row_s = lax.broadcasted_iota(jnp.int32, shape, 2).astype(F32)
        for zs in range(layers):
            info = pk[(z - zs + layers) % layers]
            named = jnp.zeros((plane, rows), F32)
            gate = jnp.zeros((plane, rows), F32)
            for k in range(top):
                same = info[k : k + 1, :] == expert
                named = named + jnp.where(same, 1.0, 0.0)
                gate = gate + jnp.where(same, info[top + k : top + k + 1, :], 0.0)
            rank = jnp.dot(named.astype(BF), upper, preferred_element_type=F32)
            rank = jnp.where(named > 0.5, rank, -1.0)
            full = (row_s == rank[:, None, None, :]) & (row_z == zs)
            one = jnp.where(full, 1.0, 0.0).reshape(slots, rows)
            pmat[:, zs * rows : (zs + 1) * rows] = one.astype(BF)
            wt = jnp.where(full, gate[:, None, None, :], 0.0).reshape(slots, rows).T
            hi = wt.astype(BF)
            chi[zs * rows : (zs + 1) * rows, :] = hi
            clo[zs * rows : (zs + 1) * rows, :] = (wt - hi.astype(F32)).astype(BF)

    for c in range(chunks):
        own_copy(c).wait()
    start_hop(0, 1)
    start_hop(1, 1)
    masks()
    acc_g[...] = jnp.zeros_like(acc_g)
    acc_u[...] = jnp.zeros_like(acc_u)
    acc_h[...] = jnp.zeros_like(acc_h)
    last = (((1,), (1,)), ((), ()))
    tile = 256

    def step(i, _):
        @pl.when(jnp.logical_and(i >= 2, i < chunks))
        def _():
            start_hop(i, 1)

        for h in range(1, layers):
            c = i - h

            @pl.when(jnp.logical_and(c >= 0, c < chunks))
            def _():
                wait_hop(c, h)
                if h < layers - 1:
                    start_hop(c, h + 1)

        c = i - (layers - 1)

        @pl.when(jnp.logical_and(c >= 0, c < chunks))
        def _():
            slot = c % per

            @pl.when(c >= per)
            def _():
                remote(
                    group(snd.at[slot]), group(snd.at[slot]), snd_ss.at[c - per],
                    rcv_rs.at[c - per], dev(z, (q + 1) % plane),
                ).wait_send()

            built = jnp.dot(pmat[...], ag[c].reshape(toks, cw), preferred_element_type=F32)
            built = built.astype(BF).reshape(plane, blk, cw)
            snd[slot] = built
            rcv[c, 0] = built[0]
            plane_send(snd.at[slot], rcv.at[c], snd_ss.at[c], rcv_rs.at[c], 1)

        c2 = i - (layers + 1)

        @pl.when(c2 >= 0)
        def _():
            remote(
                group(rcv.at[c2]), group(rcv.at[c2]), snd_ss.at[c2], rcv_rs.at[c2],
                dev(z, (q + 1) % plane),
            ).wait_recv()
            ws = c2 % 2

            @pl.when(c2 < per)
            def _():
                for cp in w_copies(c2, ws):
                    cp.wait()

                @pl.when(c2 + 1 < per)
                def _():
                    for cp in w_copies(c2 + 1, (c2 + 1) % 2):
                        cp.start()

                @pl.loop(0, hidden // tile)
                def _(t):
                    at = pl.ds(pl.multiple_of(t * tile, tile), tile)
                    xr = rcv[c2].reshape(slots, cw)
                    acc_g[:, at] += jnp.dot(xr, wgs[ws, :, at], preferred_element_type=F32)
                    acc_u[:, at] += jnp.dot(xr, wus[ws, :, at], preferred_element_type=F32)

            @pl.when(c2 >= per)
            def _():
                c3 = c2 - per
                wd_copy(c3, c3 % 2).wait()

                @pl.when(c3 + 1 < per)
                def _():
                    wd_copy(c3 + 1, (c3 + 1) % 2).start()

                @pl.when(c3 == 0)
                def _():
                    for cp in w_copies(0, 0):
                        cp.start()

                @pl.loop(0, hidden // tile)
                def _(t):
                    at = pl.ds(pl.multiple_of(t * tile, tile), tile)
                    dr = rcv[c2].reshape(slots, cw)
                    acc_h[:, at] += lax.dot_general(
                        dr, wds[c3 % 2, at, :], last, preferred_element_type=F32
                    )

        return 0

    lax.fori_loop(0, chunks + layers + 1, step, 0)

    for cp in w_copies(0, 0):
        cp.wait()
    for cp in w_copies(1, 1):
        cp.start()
    remote(
        group(snd.at[0]), group(snd.at[0]), snd_ss.at[per], rcv_rs.at[per],
        dev(z, (q + 1) % plane),
    ).wait_send()
    for j in list(range(1, plane)) + [0]:
        at = pl.ds(j * blk, blk)
        g, u, d = acc_g[at, :], acc_u[at, :], acc_h[at, :]
        sig = jax.nn.sigmoid(g)
        act = g * sig
        score = jnp.sum(act * u * d, axis=1, keepdims=True)
        sc[j] = jnp.broadcast_to(score, (blk, rows)).astype(BF)
        ggp[at, :] = (d * u * sig * (1.0 + g * (1.0 - sig))).astype(BF)
        gup[at, :] = (d * act).astype(BF)
        grad = lax.dot_general(ggp[at, :], wgs[0], last, preferred_element_type=F32)
        grad = grad + lax.dot_general(gup[at, :], wus[0], last, preferred_element_type=F32)
        snd[0, j] = grad.astype(BF)
        if j == 0:
            rcv[0, 0] = grad.astype(BF)
        else:
            remote(
                snd.at[0, j], rcv.at[0, j], ret_ss.at[0], ret_rs.at[0],
                dev(z, (q - j + plane) % plane),
            ).start()

    scr[0] = sc[0]
    plane_send(sc, scr, mis_ss.at[1], mis_rs.at[1], -1)

    outer = jnp.logical_or(z == 0, z == layers - 1)
    inner = jnp.logical_not(outer)
    beside = z + 1 - 2 * (z % 2)
    across, far = layers - 1 - z, layers - 1 - beside

    def to_layer(c, block, slot, who, turn):
        return remote(
            zsnd.at[c, block], zrcv.at[c, slot], z_ss.at[c, turn], z_rs.at[c, turn], dev(who, q)
        )

    def landed(c, start, count, turn):
        some = zrcv.at[c, pl.ds(start, count)]
        return remote(some, some, z_ss.at[c, turn], z_rs.at[c, turn], dev(beside, q))

    def first_hop(c):
        to_layer(c, beside, 0, beside, 0).start()

        @pl.when(outer)
        def _():
            to_layer(c, far, 1, beside, 0).start()
            to_layer(c, across, 2, beside, 0).start()

    def second_hop(c):
        landed(c, 0, 3, 0).wait_recv()
        for block, slot in ((across, 1), (far, 2)):
            both = zsnd[c, block].astype(F32) + zrcv[c, slot].astype(F32)
            zsnd[c, block] = both.astype(BF)
            to_layer(c, block, 3, block, 1).start()

    def back(i, _):
        @pl.when(i < per)
        def _():
            ws = i % 2
            for cp in w_copies(i, ws):
                cp.wait()

            @pl.when(i + 1 < per)
            def _():
                for cp in w_copies(i + 1, (i + 1) % 2):
                    cp.start()

            remote(
                group(snd.at[i]), group(snd.at[i]), snd_ss.at[per + i], rcv_rs.at[per + i],
                dev(z, (q + 1) % plane),
            ).wait_send()
            grad = lax.dot_general(ggp[...], wgs[ws], last, preferred_element_type=F32)
            grad = grad + lax.dot_general(gup[...], wus[ws], last, preferred_element_type=F32)
            out = grad.astype(BF).reshape(plane, blk, cw)
            snd[i] = out
            rcv[i, 0] = out[0]
            plane_send(snd.at[i], rcv.at[i], ret_ss.at[i], ret_rs.at[i], -1)

        c = i - 2

        @pl.when(jnp.logical_and(c >= 0, c < per))
        def _():
            done = remote(
                group(rcv.at[c]), group(rcv.at[c]), ret_ss.at[c], ret_rs.at[c],
                dev(z, (q + 1) % plane),
            )
            done.wait_send()
            done.wait_recv()
            rr = rcv[c].reshape(slots, cw)
            part = jnp.dot(chi[...], rr, preferred_element_type=F32)
            part = part + jnp.dot(clo[...], rr, preferred_element_type=F32)
            zsnd[c] = part.astype(BF).reshape(layers, rows, cw)
            first_hop(c)

        b = i - 3

        @pl.when(jnp.logical_and(b >= 0, inner))
        def _():
            second_hop(b)

        return 0

    lax.fori_loop(1, per + 3, back, 0)

    wait_both(group(scr), mis_ss.at[1], mis_rs.at[1])
    jj = lax.broadcasted_iota(jnp.int32, (plane, rows), 0)
    expert = (z * plane + (q + jj) % plane).astype(F32)
    val = scr[...].astype(F32).reshape(slots, rows)
    for zs in range(layers):
        info = pk[(z - zs + layers) % layers]
        hold = pmat[:, zs * rows : (zs + 1) * rows].astype(F32) * val
        by = jnp.sum(hold.reshape(plane, blk, rows), axis=1)
        parts = [
            jnp.sum(jnp.where(info[k : k + 1, :] == expert, by, 0.0), axis=0, keepdims=True)
            for k in range(top)
        ]
        gz[zs] = jnp.concatenate(parts + [jnp.zeros((8 - top, rows), F32)], axis=0)
    z_all(lambda r: gz.at[(z + r) % layers], gzr, mis_ss.at[2], mis_rs.at[2])

    for c in range(per):
        @pl.when(outer)
        def _():
            landed(c, 0, 1, 0).wait_recv()
            landed(c, 0, 3, 0).wait_send()

        @pl.when(inner)
        def _():
            landed(c, 0, 1, 0).wait_send()
            landed(c, 0, 2, 1).wait_send()

        landed(c, 3, 1, 1).wait_recv()
        total = zsnd[c, z].astype(F32) + zrcv[c, 0].astype(F32) + zrcv[c, 3].astype(F32)
        tg_ref[:, c * cw : (c + 1) * cw] = total.astype(BF)

    wait_both(gzr.at[pl.ds(1, layers - 1)], mis_ss.at[2], mis_rs.at[2])
    total = gz[z]
    for r in range(1, layers):
        total = total + gzr[r]
    gg_ref[...] = total

    def drain(c, _):
        for h in range(1, layers):
            for way in (1, -1):
                @pl.when(sends(h, way))
                def _():
                    hop(c, h, way).wait_send()
        return 0

    lax.fori_loop(0, chunks, drain, 0)


def plane_body(tokens, out_grad, route_ids, route_gates, w_gate, w_up, w_down):
    n = lax.axis_size("expert")
    plane = 8
    layers = n // plane
    rows, width = tokens.shape
    hidden = w_gate.shape[2]
    top = route_ids.shape[1]
    cap = 3 * rows * top // (2 * n)
    cw = 512
    per = width // cw
    blk = layers * cap
    slots = plane * blk
    toks = layers * rows
    packed = jnp.concatenate([route_ids.astype(F32), route_gates], axis=1).T
    vm = pl.BlockSpec(memory_space=pltpu.VMEM)
    hbm = pl.BlockSpec(memory_space=pl.ANY)
    dma = pltpu.SemaphoreType.DMA
    token_grad, gates_t = pl.pallas_call(
        functools.partial(fused_kernel, layers, plane, rows, cap, width, hidden, top, cw),
        out_shape=(
            jax.ShapeDtypeStruct((rows, width), BF),
            jax.ShapeDtypeStruct((8, rows), F32),
        ),
        in_specs=[vm, hbm, hbm, hbm, hbm, hbm],
        out_specs=(vm, vm),
        scratch_shapes=[
            pltpu.VMEM((layers, 8, rows), F32),
            pltpu.VMEM((2 * per, layers, rows, cw), BF),
            pltpu.VMEM((per, plane, blk, cw), BF),
            pltpu.VMEM((2 * per, plane, blk, cw), BF),
            pltpu.VMEM((per, layers, rows, cw), BF),
            pltpu.VMEM((per, layers, rows, cw), BF),
            pltpu.VMEM((layers, 8, rows), F32),
            pltpu.VMEM((layers, 8, rows), F32),
            pltpu.VMEM((plane, blk, rows), BF),
            pltpu.VMEM((plane, blk, rows), BF),
            pltpu.VMEM((slots, toks), BF),
            pltpu.VMEM((toks, slots), BF),
            pltpu.VMEM((toks, slots), BF),
            pltpu.VMEM((slots, hidden), F32),
            pltpu.VMEM((slots, hidden), F32),
            pltpu.VMEM((slots, hidden), F32),
            pltpu.VMEM((slots, hidden), BF),
            pltpu.VMEM((slots, hidden), BF),
            pltpu.VMEM((2, cw, hidden), BF),
            pltpu.VMEM((2, cw, hidden), BF),
            pltpu.VMEM((2, hidden, cw), BF),
            dma((2 * per,)),
            dma((2 * per, layers - 1, 2)),
            dma((2 * per, layers - 1, 2)),
            dma((2 * per,)),
            dma((2 * per,)),
            dma((per,)),
            dma((per,)),
            dma((per, 2)),
            dma((per, 2)),
            dma((3,)),
            dma((3,)),
            dma((3, 2)),
        ],
        compiler_params=pltpu.CompilerParams(
            collective_id=0, has_side_effects=True, vmem_limit_bytes=64 * 1024 * 1024 - 65536
        ),
        cost_estimate=pl.CostEstimate(
            flops=10 * slots * width * hidden, bytes_accessed=10 * width * hidden, transcendentals=0
        ),
    )(packed, tokens, out_grad, w_gate[0], w_up[0], w_down[0])
    return (token_grad, gates_t[:top].T.astype(BF))


def solution(mesh):
    n = mesh.shape["expert"]
    flat = mesh.shape["hid"] != 1 or n != 32
    return jax.shard_map(
        flat_body if flat else plane_body,
        mesh=mesh,
        in_specs=(
            P("expert", None),
            P("expert", None),
            P("expert", None),
            P("expert", None),
            P("expert", None, "hid"),
            P("expert", None, "hid"),
            P("expert", "hid", None),
        ),
        out_specs=(P("expert", "hid"), P("expert", None)),
        check_vma=False,
    )
```
